32 devices in a mesh: grp: 4 (over x, core), blk: 4 (over z), sub: 2 (over y).
Axes of the slice: x: 2, y: 2, z: 4, core: 2. Of those that a mesh axis runs over, the one named last changes fastest.
Arguments:
- clips: bfloat16 [512, 128, 512], P(('grp', 'blk', 'sub')), may hold values from -6 to 6
- lengths: int32 [512], P(('grp', 'blk', 'sub')), may hold values from 32 to 128, as said below
- assign: int32 [16, 32], P(('grp', 'blk'), 'sub'), may hold values from 0 to 31, each once within a row
- text: bfloat16 [512, 1024], P(('grp', 'blk', 'sub')), may hold values from -6 to 6
- positives: int32 [4, 128], P('grp', ('blk', 'sub')), may hold values from 0 to 127, each once within a row
- conv_w: bfloat16 [1536, 512], replicated, may hold values from -0.15625 to 0.15625
- proj_w: bfloat16 [512, 1024], replicated, may hold values from -0.25 to 0.25
- logit_scale: float32 [], replicated, may hold values from 4 to 12
- logit_bias: float32 [], replicated, may hold values from -3 to -1
Outputs:
- audio_grad: float32 [512, 1024], P(('grp', 'blk', 'sub'))
- text_grad: float32 [512, 1024], P(('grp', 'blk', 'sub'))
The draws below stay inside these ranges and needn't reach their ends.
Inputs may be any that keep to these rules, and one draw needn't show every extreme that they name: `lengths`: frames at or beyond a clip's length are padding; some clip has 128 frames. `assign`: each row lists each of its pair's 2 * 16 clips once; the first device of the pair takes the first 16 entries. `positives`: each row is a permutation: every text of a group is the match of exactly one audio slot of that group.
All inputs are finite; a program needn't handle non-finite values.
Results may differ from the reference program's by a relative error of at most 0.0045.
Values may be sent and summed in bfloat16 or wider, within the bound.
No kernel may reach another device: no remote copies, remote signals or barrier semaphores. Data moves between devices by JAX's collectives and lax.ppermute only.
A program may use at most 64 MiB of HBM per device.

```python
import math
import jax
import jax.numpy as jnp
from jax import lax

CH = 512
E = 1024
ROWS = 16
FRAMES = 128
GROUP_ROWS = 128
BATCH = 512
PAIRS = 16
N_GRP = 4


def draw_lengths(key, part):
    base = jax.random.randint(jax.random.fold_in(key, 11), (BATCH,), FRAMES // 4, FRAMES + 1)
    spot = jax.random.randint(jax.random.fold_in(key, 12), (), 0, BATCH)
    return jnp.where(jnp.arange(BATCH) == spot, FRAMES, base).astype(jnp.int32)


def draw_clips(key, part):
    frame_key = jax.random.fold_in(key, 21)
    offset_key = jax.random.fold_in(key, 22)
    offset = 1.5 * jax.random.normal(offset_key, (BATCH, 1, CH), jnp.float32)
    frames = jax.random.normal(frame_key, (BATCH, FRAMES, CH), jnp.float32)
    values = frames + offset
    return jnp.clip(values, -6.0, 6.0).astype(jnp.bfloat16)


def shard_levels(rng, dims, split, least, top_value):
    factor_of, own = 1.0, jax.random.fold_in(rng, 6)
    for position, parts in split:
        draws = jnp.exp(jax.random.uniform(jax.random.fold_in(own, position), (parts,), jnp.float32, least / len(split), top_value / len(split)))
        factor_of = factor_of * jnp.repeat(draws, dims[position] // parts).reshape([-1 if axis == position else 1 for axis in range(len(dims))])
    return factor_of


def scatter_about(stream_key, dims, scale, bound, split=(), kind=jnp.bfloat16):
    gain = shard_levels(stream_key, dims, split, -0.22, 0.18) if split else 1.0
    array = jax.random.normal(stream_key, dims, jnp.float32) * scale * gain
    return jnp.minimum(jnp.maximum(array, -bound), bound).astype(kind)


def setup_inputs(seed: int = 0) -> dict:
    seeds = jax.random.split(jax.random.key(seed), 10)
    clips = draw_clips(jax.random.fold_in(seeds[9], 71), 0)
    lengths = draw_lengths(jax.random.fold_in(seeds[9], 71), 0)
    assign = jax.vmap(lambda own: jax.random.permutation(own, 2 * ROWS))(jax.random.split(seeds[2], PAIRS)).reshape((PAIRS, 2 * ROWS)).astype(jnp.int32)
    text = scatter_about(seeds[3], (BATCH, E), 1.0, 6.0, ((0, 32),))
    positives = jax.vmap(lambda own: jax.random.permutation(own, GROUP_ROWS))(jax.random.split(seeds[4], N_GRP)).reshape((N_GRP, GROUP_ROWS)).astype(jnp.int32)
    conv_w = scatter_about(seeds[5], (3 * CH, CH), (3 * CH) ** -0.5, 0.15625)
    proj_w = scatter_about(seeds[6], (CH, E), CH ** -0.5, 0.25)
    logit_scale = jnp.clip(jnp.exp(jax.random.uniform(seeds[7], (), jnp.float32, math.log(4.0), math.log(12.0))), 4.0, 12.0)
    logit_bias = jnp.clip(jax.random.uniform(seeds[8], (), jnp.float32, -3.0, -1.0), -3.0, -1.0)
    return {"clips": clips, "lengths": lengths, "assign": assign, "text": text, "positives": positives, "conv_w": conv_w, "proj_w": proj_w, "logit_scale": logit_scale, "logit_bias": logit_bias}


def tower(clips, lengths, conv_w, proj_w):
    count_frames = clips.shape[1]
    half = count_frames // 2
    frame_ids = jnp.arange(count_frames, dtype=jnp.int32)
    inside = (frame_ids[None, :] < lengths[:, None])[:, :, None]
    kept = jnp.where(inside, clips, jnp.zeros((), clips.dtype))
    padded = jnp.pad(kept, ((0, 0), (1, 0), (0, 0)))
    stacked = jnp.concatenate([padded[:, 0:count_frames:2], padded[:, 1:count_frames:2], padded[:, 2:count_frames + 1:2]], axis=2)
    hidden = jax.nn.gelu(jnp.dot(stacked.reshape(-1, stacked.shape[2]), conv_w, preferred_element_type=jnp.float32))
    hidden = hidden.reshape(clips.shape[0], half, -1)
    out_ids = jnp.arange(half, dtype=jnp.int32)
    valid = (2 * out_ids[None, :] < lengths[:, None])[:, :, None]
    counts = ((lengths + 1) // 2).astype(jnp.float32)
    pooled = (lax.optimization_barrier(jnp.sum(jnp.where(valid, hidden, jnp.zeros((), hidden.dtype)), axis=1)) / counts[:, None]).astype(jnp.bfloat16)
    projected = jnp.dot(pooled, proj_w, preferred_element_type=jnp.float32)
    return (projected * lax.rsqrt(lax.optimization_barrier(jnp.sum(projected * projected, axis=1, keepdims=True)) + 1e-06)).astype(jnp.bfloat16)

def normalize(values):
    wide = values.astype(jnp.float32)
    return (wide * lax.rsqrt(lax.optimization_barrier(jnp.sum(wide * wide, axis=1, keepdims=True)) + 1e-06)).astype(jnp.bfloat16)

def reference(clips, lengths, assign, text, positives, conv_w, proj_w, logit_scale, logit_bias):
    pair_clips = clips.reshape(PAIRS, 2 * ROWS, FRAMES, CH)
    pair_lengths = lengths.reshape(PAIRS, 2 * ROWS)

    def one_pair(items):
        group_clips, group_lengths, order = items
        embedded = tower(group_clips, group_lengths, conv_w, proj_w)
        return embedded[order]
    audio = lax.map(one_pair, (pair_clips, pair_lengths, assign)).reshape(N_GRP, GROUP_ROWS, E)
    texts = normalize(text).reshape(N_GRP, GROUP_ROWS, E)
    before = jnp.roll(texts, 1, axis=0)

    def one_group(items):
        block, own_text, prev_text, matches = items
        own_logits = logit_scale * jnp.dot(block, own_text.T, preferred_element_type=jnp.float32) + logit_bias
        next_logits = logit_scale * jnp.dot(block, prev_text.T, preferred_element_type=jnp.float32) + logit_bias
        hit = jnp.arange(GROUP_ROWS, dtype=jnp.int32)[None, :] == matches[:, None]
        own_weights = jnp.where(hit, -jax.nn.sigmoid(-own_logits), jax.nn.sigmoid(own_logits)).astype(jnp.bfloat16)
        next_weights = jax.nn.sigmoid(next_logits).astype(jnp.bfloat16)
        audio_part = logit_scale * (jnp.dot(own_weights, own_text, preferred_element_type=jnp.float32) + jnp.dot(next_weights, prev_text, preferred_element_type=jnp.float32))
        own_part = logit_scale * jnp.dot(own_weights.T, block, preferred_element_type=jnp.float32)
        next_part = logit_scale * jnp.dot(next_weights.T, block, preferred_element_type=jnp.float32)
        return (audio_part, own_part, next_part)
    audio_grad, own_part, next_part = lax.map(one_group, (audio, texts, before, positives))
    text_grad = own_part + jnp.roll(next_part, -1, axis=0)
    return (audio_grad.reshape(BATCH, E), text_grad.reshape(BATCH, E))
```

```python
import functools

import jax
import jax.numpy as jnp
from jax import lax
from jax.experimental import pallas as pl
from jax.experimental.pallas import tpu as pltpu
from jax.sharding import PartitionSpec as P

BF16 = jnp.bfloat16
F32 = jnp.float32
LANES = 128
SMEM = pl.BlockSpec(memory_space=pltpu.SMEM)
VMEM = pl.BlockSpec(memory_space=pltpu.VMEM)
PARAMS = pltpu.CompilerParams(vmem_limit_bytes=48 * 2**20)


def swapped(block, axis, bit):
    devices = range(lax.axis_size(axis))
    return lax.ppermute(block, axis, [(i, i ^ bit) for i in devices])


def passed_along(block, axis, distance):
    devices = range(lax.axis_size(axis))
    return lax.ppermute(block, axis, [((i - distance) % len(devices), i) for i in devices])


def bits_of(size):
    assert size & (size - 1) == 0
    return [1 << k for k in reversed(range(size.bit_length() - 1))]


def doubled(block, axis, bits):
    for bit in bits:
        block = jnp.concatenate([block, swapped(block, axis, bit)], axis=0)
    return block


def gelu(x):
    return x * (0.5 + 0.5 * jnp.tanh(x * (0.7978845608028654 + 0.035677408136300125 * (x * x))))


def as_column(row):
    size = row.shape[1]
    at = lax.broadcasted_iota(jnp.int32, (size, size), 0)
    lane = lax.broadcasted_iota(jnp.int32, (size, size), 1)
    return jnp.sum(jnp.where(at == lane, jnp.broadcast_to(row, (size, size)), 0.0), 1, keepdims=True)


def as_row(column):
    size = column.shape[0]
    at = lax.broadcasted_iota(jnp.int32, (size, size), 0)
    lane = lax.broadcasted_iota(jnp.int32, (size, size), 1)
    return jnp.sum(jnp.where(at == lane, jnp.broadcast_to(column, (size, size)), 0.0), 0, keepdims=True)


def product(a, b, b_axis=0):
    return lax.dot_general(a, b, (((1,), (b_axis,)), ((), ())), preferred_element_type=F32)


def tower_kernel(lengths, clips, assign, positives, conv_w, out, wide, stacked):
    count, frames, channels = clips.shape
    half = frames // 2
    rows = lax.broadcasted_iota(jnp.int32, (half, 1), 0)
    wide[:, :, 0:8, :] = jnp.zeros((wide.shape[0], channels // LANES, 8, LANES), F32)
    for c in range(count):
        inside = 2 * rows + 1 < lengths[c]
        base = c * half
        buffer = wide.at[c % wide.shape[0]]
        for k in range(channels // LANES):
            buffer[k, 8 : 8 + frames, :] = clips[c, :, k * LANES : (k + 1) * LANES].astype(F32)
        for k in range(channels // LANES):
            strip = buffer.at[k]
            taps = (
                strip[pl.ds(7, half, stride=2), :],
                strip[pl.ds(8, half, stride=2), :],
                jnp.where(inside, strip[pl.ds(9, half, stride=2), :], 0.0),
            )
            for tap, values in enumerate(taps):
                first = tap * channels + k * LANES
                stacked[base : base + half, first : first + LANES] = values.astype(BF16)
    hidden = gelu(product(stacked[...], conv_w[...]))
    pooled = []
    for c in range(count):
        valid = 2 * rows < lengths[c]
        total = jnp.sum(
            jnp.where(valid, hidden[c * half : (c + 1) * half], 0.0), axis=0, keepdims=True
        )
        pooled.append(total / ((lengths[c] + 1) // 2).astype(F32))
    out[:, 0:channels] = jnp.concatenate(pooled, axis=0).astype(BF16)
    slots = as_column(assign[...].astype(F32))
    low = as_column((positives[...] & 255).astype(F32))
    high = as_column((positives[...] >> 8).astype(F32))
    lane = lax.broadcasted_iota(jnp.int32, (count, LANES), 1)
    marks = jnp.where(lane == 0, slots, jnp.where(lane == 1, low, jnp.where(lane == 2, high, 0.0)))
    out[:, channels : channels + LANES] = marks.astype(BF16)


def normalized(wide):
    return (wide * lax.rsqrt(jnp.sum(wide * wide, axis=1, keepdims=True) + 1e-06)).astype(BF16)


def weights(logits, hit):
    return jnp.where(hit, -jax.nn.sigmoid(-logits), jax.nn.sigmoid(logits)).astype(BF16)


def logits_kernel(
    bits, place, scale, bias, gathered, proj_w, texts, next_out, peer_out, text_out, audio_out
):
    channels = proj_w.shape[0]
    rows = gathered.shape[0]
    count = text_out.shape[0]
    blk, sub = place[0], place[1]
    ls, lb = scale[0], bias[0]
    marks = gathered[:, channels : channels + LANES].astype(F32)
    slot = marks[:, 0:1].astype(jnp.int32)
    match = marks[:, 1:2] + 256.0 * marks[:, 2:3]
    here = lax.broadcasted_iota(jnp.int32, (rows, 1), 0)
    other = jnp.where(slot < count, slot + count, slot - count)
    source = here // (2 * count) * (2 * count) + jnp.where(sub == 1, other, slot)
    lane = lax.broadcasted_iota(jnp.int32, (rows, rows), 1)
    pick = jnp.where(lane == source, 1.0, 0.0).astype(BF16)
    pooled = product(pick, gathered[:, 0:channels]).astype(BF16)
    audio = normalized(product(pooled, proj_w[...]))
    zt = normalized(texts[...].astype(F32))

    near = zt[0 : 2 * count]
    logits = ls * product(near, audio, 1) + lb
    at = lax.broadcasted_iota(jnp.int32, (2 * count, 1), 0)
    wanted = jnp.where(at < count, (blk * 2 + sub) * count + at, -1).astype(F32)
    pulled = ls * product(weights(logits, wanted == as_row(match)), audio)
    next_out[...] = pulled[count:].astype(BF16)
    text_out[...] = pulled[:count]

    pair = audio[0 : 2 * count]
    logits = ls * product(pair, zt, 1) + lb
    column = lax.broadcasted_iota(jnp.int32, (1, zt.shape[0]), 1)
    step = column // count
    away = jnp.zeros_like(column)
    for k, bit in enumerate(bits):
        away = away + ((step >> (k + 1)) & 1) * bit
    wanted = jnp.where((step & 1) == 0, ((blk ^ away) * 2 + sub) * count + column % count, -1)
    pushed = ls * product(weights(logits, wanted.astype(F32) == match[0 : 2 * count]), zt)
    peer_out[...] = pushed[count:].astype(BF16)
    audio_out[...] = pushed[:count]


def sum_kernel(audio, peer, text, after, audio_grad, text_grad):
    audio_grad[...] = audio[...] + peer[...].astype(F32)
    text_grad[...] = text[...] + after[...].astype(F32)


def on_device(clips, lengths, assign, text, positives, conv_w, proj_w, logit_scale, logit_bias):
    count, frames, channels = clips.shape
    width = text.shape[1]
    assert lax.axis_size("sub") == 2 and count <= 128
    bits = bits_of(lax.axis_size("blk"))
    texts = jnp.concatenate([text, passed_along(text, "grp", 1)], axis=0)
    texts = doubled(texts, "blk", bits)
    own = pl.pallas_call(
        tower_kernel,
        out_shape=jax.ShapeDtypeStruct((count, channels + LANES), BF16),
        in_specs=[SMEM, VMEM, VMEM, VMEM, VMEM],
        out_specs=VMEM,
        scratch_shapes=[
            pltpu.VMEM((2, channels // LANES, 8 + frames, LANES), F32),
            pltpu.VMEM((count * frames // 2, 3 * channels), BF16),
        ],
        compiler_params=PARAMS,
        cost_estimate=pl.CostEstimate(flops=count * frames * 3 * channels * channels, bytes_accessed=clips.size * 4, transcendentals=count * frames * channels // 2),
        name="tower",
    )(lengths, clips, assign, positives, conv_w)
    gathered = doubled(doubled(own, "sub", [1]), "blk", bits)
    place = jnp.stack([lax.axis_index("blk"), lax.axis_index("sub")]).astype(jnp.int32)
    block = (count, width)
    after, peer, text_part, audio_part = pl.pallas_call(
        functools.partial(logits_kernel, bits),
        out_shape=[jax.ShapeDtypeStruct(block, t) for t in (BF16, BF16, F32, F32)],
        in_specs=[SMEM, SMEM, SMEM, VMEM, VMEM, VMEM],
        out_specs=[VMEM] * 4,
        compiler_params=PARAMS,
        name="logits",
    )(place, logit_scale.reshape(1), logit_bias.reshape(1), gathered, proj_w, texts)
    after = passed_along(after, "grp", -1)
    peer = swapped(peer, "sub", 1)
    return pl.pallas_call(
        sum_kernel,
        out_shape=[jax.ShapeDtypeStruct(block, F32)] * 2,
        in_specs=[VMEM] * 4,
        out_specs=[VMEM] * 2,
        compiler_params=PARAMS,
        name="sums",
    )(audio_part, peer, text_part, after)


def solution(mesh):
    in_specs = (
        P(("grp", "blk", "sub"), None, None),
        P(("grp", "blk", "sub")),
        P(("grp", "blk"), "sub"),
        P(("grp", "blk", "sub"), None),
        P("grp", ("blk", "sub")),
        P(),
        P(),
        P(),
        P(),
    )
    out_specs = (P(("grp", "blk", "sub"), None), P(("grp", "blk", "sub"), None))
    return jax.shard_map(
        on_device, mesh=mesh, in_specs=in_specs, out_specs=out_specs, check_vma=False
    )
```

```python
import functools

import jax
import jax.numpy as jnp
from jax import lax
from jax.experimental import pallas as pl
from jax.experimental.pallas import tpu as pltpu
from jax.sharding import PartitionSpec as P

BF16 = jnp.bfloat16
F32 = jnp.float32
LANES = 128
SMEM = pl.BlockSpec(memory_space=pltpu.SMEM)
VMEM = pl.BlockSpec(memory_space=pltpu.VMEM)
HBM = pl.BlockSpec(memory_space=pltpu.HBM)
PARAMS = pltpu.CompilerParams(vmem_limit_bytes=48 * 2**20)


def swapped(block, axis, bit):
    devices = range(lax.axis_size(axis))
    return lax.ppermute(block, axis, [(i, i ^ bit) for i in devices])


def passed_along(block, axis, distance):
    devices = range(lax.axis_size(axis))
    return lax.ppermute(block, axis, [((i - distance) % len(devices), i) for i in devices])


def bits_of(size):
    assert size & (size - 1) == 0
    return [1 << k for k in reversed(range(size.bit_length() - 1))]


def doubled(block, axis, bits):
    for bit in bits:
        block = jnp.concatenate([block, swapped(block, axis, bit)], axis=0)
    return block


def gelu(x):
    return x * (0.5 + 0.5 * jnp.tanh(x * (0.7978845608028654 + 0.035677408136300125 * (x * x))))


def as_column(row):
    size = row.shape[1]
    at = lax.broadcasted_iota(jnp.int32, (size, size), 0)
    lane = lax.broadcasted_iota(jnp.int32, (size, size), 1)
    return jnp.sum(jnp.where(at == lane, jnp.broadcast_to(row, (size, size)), 0.0), 1, keepdims=True)


def as_row(column):
    size = column.shape[0]
    at = lax.broadcasted_iota(jnp.int32, (size, size), 0)
    lane = lax.broadcasted_iota(jnp.int32, (size, size), 1)
    return jnp.sum(jnp.where(at == lane, jnp.broadcast_to(column, (size, size)), 0.0), 0, keepdims=True)


def product(a, b, b_axis=0):
    return lax.dot_general(a, b, (((1,), (b_axis,)), ((), ())), preferred_element_type=F32)


def tower_kernel(
    lengths_in, clips_in, assign_in, positives_in, conv_in, proj_in,
    out, proj_w, lengths, clips, assign, positives, conv_w, wide, stacked, sems,
):
    count, frames, channels = clips.shape
    half = frames // 2
    parts = clips.shape[0] // 4
    copies = [pltpu.make_async_copy(lengths_in, lengths, sems.at[0])]
    for n in range(4):
        part = pl.ds(n * parts, parts)
        copies.append(pltpu.make_async_copy(clips_in.at[part], clips.at[part], sems.at[1 + n]))
    copies.append(pltpu.make_async_copy(conv_in, conv_w, sems.at[5]))
    copies.append(pltpu.make_async_copy(assign_in, assign, sems.at[6]))
    copies.append(pltpu.make_async_copy(positives_in, positives, sems.at[7]))
    copies.append(pltpu.make_async_copy(proj_in, proj_w, sems.at[8]))
    for copy in copies:
        copy.start()
    wide[:, :, 0:8, :] = jnp.zeros((wide.shape[0], channels // LANES, 8, LANES), F32)
    rows = lax.broadcasted_iota(jnp.int32, (half, 1), 0)
    copies[0].wait()
    for c in range(count):
        if c % parts == 0:
            copies[1 + c // parts].wait()
        inside = 2 * rows + 1 < lengths[c]
        base = c * half
        buffer = wide.at[c % wide.shape[0]]
        for k in range(channels // LANES):
            buffer[k, 8 : 8 + frames, :] = clips[c, :, k * LANES : (k + 1) * LANES].astype(F32)
        for k in range(channels // LANES):
            strip = buffer.at[k]
            taps = (
                strip[pl.ds(7, half, stride=2), :],
                strip[pl.ds(8, half, stride=2), :],
                jnp.where(inside, strip[pl.ds(9, half, stride=2), :], 0.0),
            )
            for tap, values in enumerate(taps):
                first = tap * channels + k * LANES
                stacked[base : base + half, first : first + LANES] = values.astype(BF16)
    for copy in copies[5:-1]:
        copy.wait()
    hidden = gelu(product(stacked[...], conv_w[...]))
    pooled = []
    for c in range(count):
        valid = 2 * rows < lengths[c]
        total = jnp.sum(
            jnp.where(valid, hidden[c * half : (c + 1) * half], 0.0), axis=0, keepdims=True
        )
        pooled.append(total / ((lengths[c] + 1) // 2).astype(F32))
    out[:, 0:channels] = jnp.concatenate(pooled, axis=0).astype(BF16)
    slots = as_column(assign[...].astype(F32))
    low = as_column((positives[...] & 255).astype(F32))
    high = as_column((positives[...] >> 8).astype(F32))
    lane = lax.broadcasted_iota(jnp.int32, (count, LANES), 1)
    marks = jnp.where(lane == 0, slots, jnp.where(lane == 1, low, jnp.where(lane == 2, high, 0.0)))
    out[:, channels : channels + LANES] = marks.astype(BF16)
    copies[-1].wait()


def normalized(wide):
    return (wide * lax.rsqrt(jnp.sum(wide * wide, axis=1, keepdims=True) + 1e-06)).astype(BF16)


def weights(logits, hit):
    return jnp.where(hit, -jax.nn.sigmoid(-logits), jax.nn.sigmoid(logits)).astype(BF16)


def text_kernel(scale, bias, gathered, proj_w, texts, after_out, text_out, pair_out):
    channels = proj_w.shape[0]
    rows = gathered.shape[0]
    count = text_out.shape[0]
    column = rows // 2
    blk, sub = lax.axis_index("blk"), lax.axis_index("sub")
    scale, bias = scale[0], bias[0]
    marks = gathered[:, channels : channels + LANES].astype(F32)
    slot = marks[:, 0:1].astype(jnp.int32)
    match = marks[:, 1:2] + 256.0 * marks[:, 2:3]
    here = lax.broadcasted_iota(jnp.int32, (rows, 1), 0)
    block = here % column // count
    source = (slot // count ^ sub) * column + block * count + slot % count
    lane = lax.broadcasted_iota(jnp.int32, (rows, rows), 1)
    pick = jnp.where(lane == source, 1.0, 0.0).astype(BF16)
    pooled = product(pick, gathered[:, 0:channels]).astype(BF16)
    audio = normalized(product(pooled, proj_w[...]))
    pair_out[0:count] = audio[0:count]
    pair_out[count:] = audio[column : column + count]
    zt = normalized(texts[0 : 2 * count].astype(F32))
    logits = scale * product(zt, audio, 1) + bias
    at = lax.broadcasted_iota(jnp.int32, (2 * count, 1), 0)
    wanted = jnp.where(at < count, (blk * 2 + sub) * count + at, -1).astype(F32)
    pulled = scale * product(weights(logits, wanted == as_row(match)), audio)
    after_out[...] = pulled[count:].astype(BF16)
    text_out[...] = pulled[:count]


def audio_kernel(bits, scale, bias, pair, gathered, texts, peer_out, audio_out):
    count = pair.shape[0] // 2
    column = gathered.shape[0] // 2
    channels = gathered.shape[1] - LANES
    blk, sub = lax.axis_index("blk"), lax.axis_index("sub")
    scale, bias = scale[0], bias[0]
    marks = jnp.concatenate(
        [gathered[0:count, channels:], gathered[column : column + count, channels:]], axis=0
    ).astype(F32)
    match = marks[:, 1:2] + 256.0 * marks[:, 2:3]
    zt = normalized(texts[...].astype(F32))
    logits = scale * product(pair[...], zt, 1) + bias
    at = lax.broadcasted_iota(jnp.int32, (1, 2 * column), 1)
    step = at // count
    away = jnp.zeros_like(at)
    for k, bit in enumerate(bits):
        away = away + ((step >> (k + 1)) & 1) * bit
    wanted = jnp.where((step & 1) == 0, ((blk ^ away) * 2 + sub) * count + at % count, -1)
    pushed = scale * product(weights(logits, wanted.astype(F32) == match), zt)
    peer_out[...] = pushed[count:].astype(BF16)
    audio_out[...] = pushed[:count]


def sum_kernel(audio, peer, text, after, audio_grad, text_grad):
    audio_grad[...] = audio[...] + peer[...].astype(F32)
    text_grad[...] = text[...] + after[...].astype(F32)


def in_hbm(array):
    return pltpu.with_memory_space_constraint(array, pltpu.HBM)


def on_device(clips, lengths, assign, text, positives, conv_w, proj_w, logit_scale, logit_bias):
    count, frames, channels = clips.shape
    width = text.shape[1]
    assert lax.axis_size("sub") == 2 and count <= 128 and count % 4 == 0
    bits = bits_of(lax.axis_size("blk"))
    before = passed_along(text, "grp", 1)
    inputs = (lengths, clips, assign, positives, conv_w, proj_w)
    own, proj_w = pl.pallas_call(
        tower_kernel,
        out_shape=[
            jax.ShapeDtypeStruct((count, channels + LANES), BF16),
            jax.ShapeDtypeStruct(proj_w.shape, BF16),
        ],
        in_specs=[HBM] * 6,
        out_specs=[VMEM] * 2,
        scratch_shapes=[
            pltpu.SMEM(lengths.shape, jnp.int32),
            pltpu.VMEM(clips.shape, BF16),
            pltpu.VMEM(assign.shape, jnp.int32),
            pltpu.VMEM(positives.shape, jnp.int32),
            pltpu.VMEM(conv_w.shape, BF16),
            pltpu.VMEM((2, channels // LANES, 8 + frames, LANES), F32),
            pltpu.VMEM((count * frames // 2, 3 * channels), BF16),
            pltpu.SemaphoreType.DMA((9,)),
        ],
        compiler_params=PARAMS,
        cost_estimate=pl.CostEstimate(
            flops=count * frames * 3 * channels * channels,
            bytes_accessed=clips.size * 4,
            transcendentals=count * frames * channels // 2,
        ),
        name="tower",
    )(*map(in_hbm, inputs))
    own, both = lax.optimization_barrier((own, jnp.concatenate([text, before], axis=0)))
    gathered = doubled(own, "blk", bits[:1])
    gathered, logit_scale, logit_bias = lax.optimization_barrier((gathered, logit_scale, logit_bias))
    gathered = doubled(doubled(gathered, "blk", bits[1:]), "sub", [1])
    texts = doubled(both, "blk", bits)
    scale, bias = logit_scale.reshape(1), logit_bias.reshape(1)
    block = (count, width)
    after, text_part, pair = pl.pallas_call(
        text_kernel,
        out_shape=[
            jax.ShapeDtypeStruct(block, BF16),
            jax.ShapeDtypeStruct(block, F32),
            jax.ShapeDtypeStruct((2 * count, width), BF16),
        ],
        in_specs=[SMEM, SMEM, VMEM, VMEM, VMEM],
        out_specs=[VMEM] * 3,
        compiler_params=PARAMS,
        name="text_side",
    )(scale, bias, gathered, proj_w, both)
    after = passed_along(after, "grp", -1)
    peer, audio_part = pl.pallas_call(
        functools.partial(audio_kernel, bits),
        out_shape=[jax.ShapeDtypeStruct(block, t) for t in (BF16, F32)],
        in_specs=[SMEM, SMEM, VMEM, VMEM, VMEM],
        out_specs=[VMEM] * 2,
        compiler_params=PARAMS,
        name="audio_side",
    )(scale, bias, pair, gathered, texts)
    peer = swapped(peer, "sub", 1)
    return pl.pallas_call(
        sum_kernel,
        out_shape=[jax.ShapeDtypeStruct(block, F32)] * 2,
        in_specs=[VMEM] * 4,
        out_specs=[VMEM] * 2,
        compiler_params=PARAMS,
        name="sums",
    )(audio_part, peer, text_part, after)


def solution(mesh):
    in_specs = (
        P(("grp", "blk", "sub"), None, None),
        P(("grp", "blk", "sub")),
        P(("grp", "blk"), "sub"),
        P(("grp", "blk", "sub"), None),
        P("grp", ("blk", "sub")),
        P(),
        P(),
        P(),
        P(),
    )
    out_specs = (P(("grp", "blk", "sub"), None), P(("grp", "blk", "sub"), None))
    return jax.shard_map(
        on_device, mesh=mesh, in_specs=in_specs, out_specs=out_specs, check_vma=False
    )
```

```python
import functools
import math

import jax
import jax.numpy as jnp
from jax import lax
from jax.experimental import pallas as pl
from jax.experimental.pallas import tpu as pltpu
from jax.sharding import PartitionSpec as P

BF16 = jnp.bfloat16
F32 = jnp.float32
LANES = 128
SMEM = pl.BlockSpec(memory_space=pltpu.SMEM)
VMEM = pl.BlockSpec(memory_space=pltpu.VMEM)
HBM = pl.BlockSpec(memory_space=pltpu.HBM)
PARAMS = pltpu.CompilerParams(vmem_limit_bytes=48 * 2**20)


def swapped(block, axis, bit):
    devices = range(lax.axis_size(axis))
    return lax.ppermute(block, axis, [(i, i ^ bit) for i in devices])


def swapped_over(block, axes, bits):
    sizes = [lax.axis_size(axis) for axis in axes]
    route = []
    for i in range(math.prod(sizes)):
        rest, away, stride = i, 0, 1
        for size, bit in zip(reversed(sizes), reversed(bits)):
            away += (rest % size ^ bit) * stride
            rest, stride = rest // size, stride * size
        route.append((i, away))
    return lax.ppermute(block, axes, route)


def passed_along(block, axis, distance):
    devices = range(lax.axis_size(axis))
    return lax.ppermute(block, axis, [((i - distance) % len(devices), i) for i in devices])


def bits_of(size):
    assert size & (size - 1) == 0
    return [1 << k for k in reversed(range(size.bit_length() - 1))]


def doubled(block, axis, bits):
    for bit in bits:
        block = jnp.concatenate([block, swapped(block, axis, bit)], axis=0)
    return block


def gelu(x):
    return x * (0.5 + 0.5 * jnp.tanh(x * (0.7978845608028654 + 0.035677408136300125 * (x * x))))


def as_column(row):
    size = row.shape[1]
    at = lax.broadcasted_iota(jnp.int32, (size, size), 0)
    lane = lax.broadcasted_iota(jnp.int32, (size, size), 1)
    return jnp.sum(jnp.where(at == lane, jnp.broadcast_to(row, (size, size)), 0.0), 1, keepdims=True)


def product(a, b, b_axis=0):
    return lax.dot_general(a, b, (((1,), (b_axis,)), ((), ())), preferred_element_type=F32)


def tower_kernel(
    lengths_in, clips_in, assign_in, positives_in, conv_in, proj_in,
    out, proj_w, lengths, clips, assign, positives, conv_w, wide, stacked, sems,
):
    count, frames, channels = clips.shape
    half = frames // 2
    parts = clips.shape[0] // 4
    copies = [pltpu.make_async_copy(lengths_in, lengths, sems.at[0])]
    for n in range(4):
        part = pl.ds(n * parts, parts)
        copies.append(pltpu.make_async_copy(clips_in.at[part], clips.at[part], sems.at[1 + n]))
    copies.append(pltpu.make_async_copy(conv_in, conv_w, sems.at[5]))
    copies.append(pltpu.make_async_copy(assign_in, assign, sems.at[6]))
    copies.append(pltpu.make_async_copy(positives_in, positives, sems.at[7]))
    copies.append(pltpu.make_async_copy(proj_in, proj_w, sems.at[8]))
    for copy in copies[:-1]:
        copy.start()
    wide[:, :, 0:8, :] = jnp.zeros((wide.shape[0], channels // LANES, 8, LANES), F32)
    rows = lax.broadcasted_iota(jnp.int32, (half, 1), 0)
    copies[0].wait()
    for c in range(count):
        if c % parts == 0:
            copies[1 + c // parts].wait()
        inside = 2 * rows + 1 < lengths[c]
        base = c * half
        buffer = wide.at[c % wide.shape[0]]
        for k in range(channels // LANES):
            buffer[k, 8 : 8 + frames, :] = clips[c, :, k * LANES : (k + 1) * LANES].astype(F32)
        for k in range(channels // LANES):
            strip = buffer.at[k]
            taps = (
                strip[pl.ds(7, half, stride=2), :],
                strip[pl.ds(8, half, stride=2), :],
                jnp.where(inside, strip[pl.ds(9, half, stride=2), :], 0.0),
            )
            for tap, values in enumerate(taps):
                first = tap * channels + k * LANES
                stacked[base : base + half, first : first + LANES] = values.astype(BF16)
    copies[-1].start()
    for copy in copies[5:-1]:
        copy.wait()
    pooled = []
    step = parts * half
    for n in range(4):
        hidden = gelu(product(stacked[n * step : (n + 1) * step], conv_w[...]))
        for c in range(parts):
            length = lengths[n * parts + c]
            valid = 2 * rows < length
            total = jnp.sum(
                jnp.where(valid, hidden[c * half : (c + 1) * half], 0.0), axis=0, keepdims=True
            )
            pooled.append(total / ((length + 1) // 2).astype(F32))
    out[:, 0:channels] = jnp.concatenate(pooled, axis=0).astype(BF16)
    slots = as_column(assign[...].astype(F32))
    low = as_column((positives[...] & 255).astype(F32))
    high = as_column((positives[...] >> 8).astype(F32))
    lane = lax.broadcasted_iota(jnp.int32, (count, LANES), 1)
    marks = jnp.where(lane == 0, slots, jnp.where(lane == 1, low, jnp.where(lane == 2, high, 0.0)))
    out[:, channels : channels + LANES] = marks.astype(BF16)
    copies[-1].wait()


def normalized(wide):
    return (wide * lax.rsqrt(jnp.sum(wide * wide, axis=1, keepdims=True) + 1e-06)).astype(BF16)


def weights(logits, hit):
    return jnp.where(hit, -jax.nn.sigmoid(-logits), jax.nn.sigmoid(logits)).astype(BF16)


def next_kernel(scale, bias, gathered, proj_w, texts, after_out, audio_out):
    count = after_out.shape[0]
    audio = normalized(product(gathered[:, 0 : proj_w.shape[0]], proj_w[...]))
    audio_out[...] = audio
    zt = normalized(texts[count:].astype(F32))
    logits = scale[0] * product(zt, audio, 1) + bias[0]
    after_out[...] = (scale[0] * product(jax.nn.sigmoid(logits).astype(BF16), audio)).astype(BF16)


def own_kernel(scale, bias, gathered, audio, texts, text_out, pair_out):
    rows = gathered.shape[0]
    count = text_out.shape[0]
    channels = gathered.shape[1] - LANES
    column = rows // 2
    blk, sub = lax.axis_index("blk"), lax.axis_index("sub")
    marks = gathered[:, channels : channels + LANES].astype(F32)
    slot = marks[:, 0:1].astype(jnp.int32)
    match = marks[:, 1:2] + 256.0 * marks[:, 2:3]
    here = lax.broadcasted_iota(jnp.int32, (rows, 1), 0)
    block = here % column // count
    source = (slot // count ^ sub) * column + block * count + slot % count
    lane = lax.broadcasted_iota(jnp.int32, (rows, rows), 1)
    picked = lane == source
    near = jnp.concatenate([picked[0:count], picked[column : column + count]], axis=0)
    pair_out[...] = product(jnp.where(near, 1.0, 0.0).astype(BF16), audio[...]).astype(BF16)
    wanted_by = jnp.sum(jnp.where(picked, jnp.broadcast_to(match, (rows, rows)), 0.0), 0, keepdims=True)
    zt = normalized(texts[0:count].astype(F32))
    logits = scale[0] * product(zt, audio[...], 1) + bias[0]
    at = lax.broadcasted_iota(jnp.int32, (count, 1), 0) + (blk * 2 + sub) * count
    text_out[...] = scale[0] * product(weights(logits, at.astype(F32) == wanted_by), audio[...])


def audio_kernel(bits, scale, bias, pair, gathered, texts, peer_out, audio_out):
    count = pair.shape[0] // 2
    column = gathered.shape[0] // 2
    channels = gathered.shape[1] - LANES
    blk, sub = lax.axis_index("blk"), lax.axis_index("sub")
    scale, bias = scale[0], bias[0]
    marks = jnp.concatenate(
        [gathered[0:count, channels:], gathered[column : column + count, channels:]], axis=0
    ).astype(F32)
    match = marks[:, 1:2] + 256.0 * marks[:, 2:3]
    zt = normalized(texts[...].astype(F32))
    logits = scale * product(pair[...], zt, 1) + bias
    at = lax.broadcasted_iota(jnp.int32, (1, 2 * column), 1)
    step = at // count
    away = jnp.zeros_like(at)
    for k, bit in enumerate(bits):
        away = away + ((step >> (k + 1)) & 1) * bit
    wanted = jnp.where((step & 1) == 0, ((blk ^ away) * 2 + sub) * count + at % count, -1)
    pushed = scale * product(weights(logits, wanted.astype(F32) == match), zt)
    peer_out[...] = pushed[count:].astype(BF16)
    audio_out[...] = pushed[:count]


def sum_kernel(audio, peer, text, after, audio_grad, text_grad):
    audio_grad[...] = audio[...] + peer[...].astype(F32)
    text_grad[...] = text[...] + after[...].astype(F32)


def in_hbm(array):
    return pltpu.with_memory_space_constraint(array, pltpu.HBM)


def tower(clips, lengths, assign, positives, conv_w, proj_w):
    count, frames, channels = clips.shape
    inputs = (lengths, clips, assign, positives, conv_w, proj_w)
    return pl.pallas_call(
        tower_kernel,
        out_shape=[
            jax.ShapeDtypeStruct((count, channels + LANES), BF16),
            jax.ShapeDtypeStruct(proj_w.shape, BF16),
        ],
        in_specs=[HBM] * 6,
        out_specs=[VMEM] * 2,
        scratch_shapes=[
            pltpu.SMEM(lengths.shape, jnp.int32),
            pltpu.VMEM(clips.shape, BF16),
            pltpu.VMEM(assign.shape, jnp.int32),
            pltpu.VMEM(positives.shape, jnp.int32),
            pltpu.VMEM(conv_w.shape, BF16),
            pltpu.VMEM((2, channels // LANES, 8 + frames, LANES), F32),
            pltpu.VMEM((count * frames // 2, 3 * channels), BF16),
            pltpu.SemaphoreType.DMA((9,)),
        ],
        compiler_params=PARAMS,
        cost_estimate=pl.CostEstimate(
            flops=count * frames * 3 * channels * channels,
            bytes_accessed=clips.size * 4,
            transcendentals=count * frames * channels // 2,
        ),
        name="tower",
    )(*map(in_hbm, inputs))


def on_device(clips, lengths, assign, text, positives, conv_w, proj_w, logit_scale, logit_bias):
    count, frames, channels = clips.shape
    width = text.shape[1]
    assert lax.axis_size("sub") == 2 and count <= 128 and count % 4 == 0
    bits = bits_of(lax.axis_size("blk"))
    before = passed_along(text, "grp", 1)
    own, proj_w = tower(clips, lengths, assign, positives, conv_w, proj_w)
    own, both = lax.optimization_barrier((own, jnp.concatenate([text, before], axis=0)))
    gathered = doubled(own, "blk", bits[:-1])
    gathered, logit_scale, logit_bias = lax.optimization_barrier(
        (gathered, logit_scale, logit_bias)
    )
    last = bits[-1:]
    gathered = jnp.concatenate(
        [
            gathered,
            swapped_over(gathered, ("blk",), last),
            swapped_over(gathered, ("sub",), [1]),
            swapped_over(gathered, ("blk", "sub"), last + [1]),
        ],
        axis=0,
    )
    texts = doubled(both, "blk", bits[:-1])
    beside = swapped(both, "blk", bits[-1])
    texts, beside = lax.optimization_barrier((texts, beside))
    texts = jnp.concatenate(
        [texts, beside, swapped(texts[2 * count :], "blk", bits[-1])], axis=0
    )
    scale, bias = logit_scale.reshape(1), logit_bias.reshape(1)
    block = (count, width)
    after, audio = pl.pallas_call(
        next_kernel,
        out_shape=[
            jax.ShapeDtypeStruct(block, BF16),
            jax.ShapeDtypeStruct((gathered.shape[0], width), BF16),
        ],
        in_specs=[SMEM, SMEM, VMEM, VMEM, VMEM],
        out_specs=[VMEM] * 2,
        compiler_params=PARAMS,
        name="next_texts",
    )(scale, bias, gathered, proj_w, both)
    text_part, pair = pl.pallas_call(
        own_kernel,
        out_shape=[
            jax.ShapeDtypeStruct(block, F32),
            jax.ShapeDtypeStruct((2 * count, width), BF16),
        ],
        in_specs=[SMEM, SMEM, VMEM, VMEM, VMEM],
        out_specs=[VMEM] * 2,
        compiler_params=PARAMS,
        name="own_texts",
    )(scale, bias, gathered, audio, both)
    after = passed_along(after, "grp", -1)
    peer, audio_part = pl.pallas_call(
        functools.partial(audio_kernel, bits),
        out_shape=[jax.ShapeDtypeStruct(block, t) for t in (BF16, F32)],
        in_specs=[SMEM, SMEM, VMEM, VMEM, VMEM],
        out_specs=[VMEM] * 2,
        compiler_params=PARAMS,
        name="audio_side",
    )(scale, bias, pair, gathered, texts)
    peer = swapped(peer, "sub", 1)
    return pl.pallas_call(
        sum_kernel,
        out_shape=[jax.ShapeDtypeStruct(block, F32)] * 2,
        in_specs=[VMEM] * 4,
        out_specs=[VMEM] * 2,
        compiler_params=PARAMS,
        name="sums",
    )(audio_part, peer, text_part, after)


def solution(mesh):
    in_specs = (
        P(("grp", "blk", "sub"), None, None),
        P(("grp", "blk", "sub")),
        P(("grp", "blk"), "sub"),
        P(("grp", "blk", "sub"), None),
        P("grp", ("blk", "sub")),
        P(),
        P(),
        P(),
        P(),
    )
    out_specs = (P(("grp", "blk", "sub"), None), P(("grp", "blk", "sub"), None))
    return jax.shard_map(
        on_device, mesh=mesh, in_specs=in_specs, out_specs=out_specs, check_vma=False
    )
```

```python
import functools
import math

import jax
import jax.numpy as jnp
from jax import lax
from jax.experimental import pallas as pl
from jax.experimental.pallas import tpu as pltpu
from jax.sharding import PartitionSpec as P

BF16 = jnp.bfloat16
F32 = jnp.float32
LANES = 128
SMEM = pl.BlockSpec(memory_space=pltpu.SMEM)
VMEM = pl.BlockSpec(memory_space=pltpu.VMEM)
HBM = pl.BlockSpec(memory_space=pltpu.HBM)
PARAMS = pltpu.CompilerParams(vmem_limit_bytes=48 * 2**20)


def swapped(block, axis, bit):
    devices = range(lax.axis_size(axis))
    return lax.ppermute(block, axis, [(i, i ^ bit) for i in devices])


def swapped_over(block, axes, bits):
    sizes = [lax.axis_size(axis) for axis in axes]
    route = []
    for i in range(math.prod(sizes)):
        rest, away, stride = i, 0, 1
        for size, bit in zip(reversed(sizes), reversed(bits)):
            away += (rest % size ^ bit) * stride
            rest, stride = rest // size, stride * size
        route.append((i, away))
    return lax.ppermute(block, axes, route)


def passed_along(block, axis, distance):
    devices = range(lax.axis_size(axis))
    return lax.ppermute(block, axis, [((i - distance) % len(devices), i) for i in devices])


def bits_of(size):
    assert size & (size - 1) == 0
    return [1 << k for k in reversed(range(size.bit_length() - 1))]


def doubled(block, axis, bits):
    for bit in bits:
        block = jnp.concatenate([block, swapped(block, axis, bit)], axis=0)
    return block


def gelu(x):
    return x * (0.5 + 0.5 * jnp.tanh(x * (0.7978845608028654 + 0.035677408136300125 * (x * x))))


def as_column(row):
    size = row.shape[1]
    at = lax.broadcasted_iota(jnp.int32, (size, size), 0)
    lane = lax.broadcasted_iota(jnp.int32, (size, size), 1)
    return jnp.sum(jnp.where(at == lane, jnp.broadcast_to(row, (size, size)), 0.0), 1, keepdims=True)


def product(a, b, b_axis=0):
    return lax.dot_general(a, b, (((1,), (b_axis,)), ((), ())), preferred_element_type=F32)


def tower_kernel(
    lengths_in, clips_in, assign_in, positives_in, conv_in, proj_in,
    out, proj_w, lengths, clips, assign, positives, conv_w, wide, stacked, sems,
):
    count, frames, channels = clips.shape
    half = frames // 2
    parts = clips.shape[0] // 4
    copies = [pltpu.make_async_copy(lengths_in, lengths, sems.at[0])]
    for n in range(4):
        part = pl.ds(n * parts, parts)
        copies.append(pltpu.make_async_copy(clips_in.at[part], clips.at[part], sems.at[1 + n]))
    copies.append(pltpu.make_async_copy(conv_in, conv_w, sems.at[5]))
    copies.append(pltpu.make_async_copy(assign_in, assign, sems.at[6]))
    copies.append(pltpu.make_async_copy(positives_in, positives, sems.at[7]))
    copies.append(pltpu.make_async_copy(proj_in, proj_w, sems.at[8]))
    for copy in copies[:-1]:
        copy.start()
    wide[:, :, 0:8, :] = jnp.zeros((wide.shape[0], channels // LANES, 8, LANES), F32)
    rows = lax.broadcasted_iota(jnp.int32, (half, 1), 0)
    copies[0].wait()
    for c in range(count):
        if c % parts == 0:
            copies[1 + c // parts].wait()
        inside = 2 * rows + 1 < lengths[c]
        base = c * half
        buffer = wide.at[c % wide.shape[0]]
        for k in range(channels // LANES):
            buffer[k, 8 : 8 + frames, :] = clips[c, :, k * LANES : (k + 1) * LANES].astype(F32)
        for k in range(channels // LANES):
            strip = buffer.at[k]
            taps = (
                strip[pl.ds(7, half, stride=2), :],
                strip[pl.ds(8, half, stride=2), :],
                jnp.where(inside, strip[pl.ds(9, half, stride=2), :], 0.0),
            )
            for tap, values in enumerate(taps):
                first = tap * channels + k * LANES
                stacked[base : base + half, first : first + LANES] = values.astype(BF16)
    copies[-1].start()
    for copy in copies[5:-1]:
        copy.wait()
    pooled = []
    step = parts * half
    for n in range(4):
        hidden = gelu(product(stacked[n * step : (n + 1) * step], conv_w[...]))
        for c in range(parts):
            length = lengths[n * parts + c]
            valid = 2 * rows < length
            total = jnp.sum(
                jnp.where(valid, hidden[c * half : (c + 1) * half], 0.0), axis=0, keepdims=True
            )
            pooled.append(total / ((length + 1) // 2).astype(F32))
    out[:, 0:channels] = jnp.concatenate(pooled, axis=0).astype(BF16)
    slots = as_column(assign[...].astype(F32))
    low = as_column((positives[...] & 255).astype(F32))
    high = as_column((positives[...] >> 8).astype(F32))
    lane = lax.broadcasted_iota(jnp.int32, (count, LANES), 1)
    marks = jnp.where(lane == 0, slots, jnp.where(lane == 1, low, jnp.where(lane == 2, high, 0.0)))
    out[:, channels : channels + LANES] = marks.astype(BF16)
    copies[-1].wait()


def normalized(wide):
    return (wide * lax.rsqrt(jnp.sum(wide * wide, axis=1, keepdims=True) + 1e-06)).astype(BF16)


def weights(logits, hit):
    return jnp.where(hit, -jax.nn.sigmoid(-logits), jax.nn.sigmoid(logits)).astype(BF16)


def embedded(pooled, proj_w):
    return normalized(product(pooled, proj_w[...]))


def pulled_by(scale, bias, texts, audio):
    zt = normalized(texts[texts.shape[0] // 2 :].astype(F32))
    logits = scale[0] * product(zt, audio, 1) + bias[0]
    return scale[0] * product(jax.nn.sigmoid(logits).astype(BF16), audio)


def next_kernel(scale, bias, *refs):
    *blocks, proj_w, texts, audio_out, after_out = refs
    channels = proj_w.shape[0]
    pooled = jnp.concatenate([block[:, 0:channels] for block in blocks], axis=0)
    audio = embedded(pooled, proj_w)
    audio_out[...] = audio
    after_out[...] = pulled_by(scale, bias, texts, audio).astype(BF16)


def own_kernel(scale, bias, *refs):
    *blocks, rows_of, texts, text_out, pair_out = refs
    count, channels = text_out.shape[0], blocks[0].shape[1] - LANES
    blk, sub = lax.axis_index("blk"), lax.axis_index("sub")
    marks = jnp.concatenate([block[:, channels:].astype(F32) for block in blocks], axis=0)
    rows = marks.shape[0]
    column = rows // 2
    audio = rows_of[...]
    slot = marks[:, 0:1].astype(jnp.int32)
    match = marks[:, 1:2] + 256.0 * marks[:, 2:3]
    here = lax.broadcasted_iota(jnp.int32, (rows, 1), 0)
    block = here % column // count
    source = (slot // count ^ sub) * column + block * count + slot % count
    lane = lax.broadcasted_iota(jnp.int32, (rows, rows), 1)
    picked = lane == source
    near = jnp.concatenate([picked[0:count], picked[column : column + count]], axis=0)
    pair_out[...] = product(jnp.where(near, 1.0, 0.0).astype(BF16), audio).astype(BF16)
    wanted_by = jnp.sum(
        jnp.where(picked, jnp.broadcast_to(match, (rows, rows)), 0.0), 0, keepdims=True
    )
    zt = normalized(texts[0:count].astype(F32))
    logits = scale[0] * product(zt, audio, 1) + bias[0]
    at = lax.broadcasted_iota(jnp.int32, (count, 1), 0) + (blk * 2 + sub) * count
    text_out[...] = scale[0] * product(weights(logits, at.astype(F32) == wanted_by), audio)


def pushed_by(bits, start, scale, bias, pair, base, opposite, texts):
    count = pair.shape[0] // 2
    channels = base.shape[1] - LANES
    blk, sub = lax.axis_index("blk"), lax.axis_index("sub")
    marks = jnp.concatenate(
        [base[0:count, channels:], opposite[0:count, channels:]], axis=0
    ).astype(F32)
    match = marks[:, 1:2] + 256.0 * marks[:, 2:3]
    zt = normalized(texts.astype(F32))
    logits = scale[0] * product(pair[...], zt, 1) + bias[0]
    at = lax.broadcasted_iota(jnp.int32, (1, texts.shape[0]), 1) + start
    step = at // count
    away = jnp.zeros_like(at)
    for k, bit in enumerate(bits):
        away = away + ((step >> (k + 1)) & 1) * bit
    wanted = jnp.where((step & 1) == 0, ((blk ^ away) * 2 + sub) * count + at % count, -1)
    return scale[0] * product(weights(logits, wanted.astype(F32) == match), zt)


def audio_kernel(
    bits, scale, bias, pair, everyone, texts, peer_out, audio_out
):
    count = pair.shape[0] // 2
    total = pushed_by(bits, 0, scale, bias, pair, everyone, everyone.at[everyone.shape[0] // 2 :], texts[...])
    peer_out[...] = total[count:].astype(BF16)
    audio_out[...] = total[:count]


def sum_kernel(audio, peer, text, after, audio_grad, text_grad):
    audio_grad[...] = audio[...] + peer[...].astype(F32)
    text_grad[...] = text[...] + after[...].astype(F32)


def in_hbm(array):
    return pltpu.with_memory_space_constraint(array, pltpu.HBM)


def tower(clips, lengths, assign, positives, conv_w, proj_w):
    count, frames, channels = clips.shape
    inputs = (lengths, clips, assign, positives, conv_w, proj_w)
    return pl.pallas_call(
        tower_kernel,
        out_shape=[
            jax.ShapeDtypeStruct((count, channels + LANES), BF16),
            jax.ShapeDtypeStruct(proj_w.shape, BF16),
        ],
        in_specs=[HBM] * 6,
        out_specs=[VMEM] * 2,
        scratch_shapes=[
            pltpu.SMEM(lengths.shape, jnp.int32),
            pltpu.VMEM(clips.shape, BF16),
            pltpu.VMEM(assign.shape, jnp.int32),
            pltpu.VMEM(positives.shape, jnp.int32),
            pltpu.VMEM(conv_w.shape, BF16),
            pltpu.VMEM((2, channels // LANES, 8 + frames, LANES), F32),
            pltpu.VMEM((count * frames // 2, 3 * channels), BF16),
            pltpu.SemaphoreType.DMA((9,)),
        ],
        compiler_params=PARAMS,
        cost_estimate=pl.CostEstimate(
            flops=count * frames * 3 * channels * channels,
            bytes_accessed=clips.size * 4,
            transcendentals=count * frames * channels // 2,
        ),
        name="tower",
    )(*map(in_hbm, inputs))


def on_device(clips, lengths, assign, text, positives, conv_w, proj_w, logit_scale, logit_bias):
    count, frames, channels = clips.shape
    width = text.shape[1]
    assert lax.axis_size("sub") == 2 and count <= 128 and count % 4 == 0
    bits = bits_of(lax.axis_size("blk"))
    before = passed_along(text, "grp", 1)
    own, proj_w = tower(clips, lengths, assign, positives, conv_w, proj_w)
    own, both = lax.optimization_barrier((own, jnp.concatenate([text, before], axis=0)))
    gathered = doubled(own, "blk", bits[:-1])
    gathered, later, logit_scale, logit_bias = lax.optimization_barrier(
        (gathered, both, logit_scale, logit_bias)
    )
    last = bits[-1:]
    corner = swapped_over(gathered, ("blk", "sub"), last + [1])
    beside_it = swapped_over(gathered, ("blk",), last)
    opposite = swapped_over(gathered, ("sub",), [1])
    texts = doubled(both, "blk", bits[:-1])
    farther = texts[2 * count :]
    texts = jnp.concatenate(
        [texts, swapped(later, "blk", bits[-1]), swapped(farther, "blk", bits[-1])], axis=0
    )
    everyone = jnp.concatenate([gathered, beside_it, opposite, corner], axis=0)
    scale, bias = logit_scale.reshape(1), logit_bias.reshape(1)
    block, double = (count, width), (2 * count, width)
    quarter = gathered.shape[0]

    def call(kernel, name, out_shape, *operands):
        return pl.pallas_call(
            kernel,
            out_shape=[jax.ShapeDtypeStruct(shape, kind) for shape, kind in out_shape],
            in_specs=[SMEM, SMEM] + [VMEM] * len(operands),
            out_specs=[VMEM] * len(out_shape),
            compiler_params=PARAMS,
            name=name,
        )(scale, bias, *operands)

    audio, after = call(
        next_kernel, "next_texts",
        [((4 * quarter, width), BF16), (block, BF16)],
        everyone, proj_w, both,
    )
    after = passed_along(after, "grp", -1)
    text_part, pair = call(
        own_kernel, "own_texts",
        [(block, F32), (double, BF16)],
        everyone, audio, both,
    )
    peer, audio_part = call(
        functools.partial(audio_kernel, bits), "audio_side",
        [(block, BF16), (block, F32)],
        pair, everyone, texts,
    )
    peer = swapped(peer, "sub", 1)
    return pl.pallas_call(
        sum_kernel,
        out_shape=[jax.ShapeDtypeStruct(block, F32)] * 2,
        in_specs=[VMEM] * 4,
        out_specs=[VMEM] * 2,
        compiler_params=PARAMS,
        name="sums",
    )(audio_part, peer, text_part, after)


def solution(mesh):
    in_specs = (
        P(("grp", "blk", "sub"), None, None),
        P(("grp", "blk", "sub")),
        P(("grp", "blk"), "sub"),
        P(("grp", "blk", "sub"), None),
        P("grp", ("blk", "sub")),
        P(),
        P(),
        P(),
        P(),
    )
    out_specs = (P(("grp", "blk", "sub"), None), P(("grp", "blk", "sub"), None))
    return jax.shard_map(
        on_device, mesh=mesh, in_specs=in_specs, out_specs=out_specs, check_vma=False
    )
```

```python
import functools
import math

import jax
import jax.numpy as jnp
from jax import lax
from jax.experimental import pallas as pl
from jax.experimental.pallas import tpu as pltpu
from jax.sharding import PartitionSpec as P

BF16 = jnp.bfloat16
F32 = jnp.float32
LANES = 128
SMEM = pl.BlockSpec(memory_space=pltpu.SMEM)
VMEM = pl.BlockSpec(memory_space=pltpu.VMEM)
HBM = pl.BlockSpec(memory_space=pltpu.HBM)
PARAMS = pltpu.CompilerParams(vmem_limit_bytes=48 * 2**20)


def swapped(block, axis, bit):
    devices = range(lax.axis_size(axis))
    return lax.ppermute(block, axis, [(i, i ^ bit) for i in devices])


def swapped_over(block, axes, bits):
    sizes = [lax.axis_size(axis) for axis in axes]
    route = []
    for i in range(math.prod(sizes)):
        rest, away, stride = i, 0, 1
        for size, bit in zip(reversed(sizes), reversed(bits)):
            away += (rest % size ^ bit) * stride
            rest, stride = rest // size, stride * size
        route.append((i, away))
    return lax.ppermute(block, axes, route)


def passed_along(block, axis, distance):
    devices = range(lax.axis_size(axis))
    return lax.ppermute(block, axis, [((i - distance) % len(devices), i) for i in devices])


def bits_of(size):
    assert size & (size - 1) == 0
    return [1 << k for k in reversed(range(size.bit_length() - 1))]


def doubled(block, axis, bits):
    for bit in bits:
        block = jnp.concatenate([block, swapped(block, axis, bit)], axis=0)
    return block


def gelu(x):
    x = x.astype(BF16)
    return (x * (BF16(0.5) + BF16(0.5) * jnp.tanh(x * (BF16(0.7978845608028654) + BF16(0.035677408136300125) * (x * x))))).astype(F32)


def as_column(row):
    size = row.shape[1]
    at = lax.broadcasted_iota(jnp.int32, (size, size), 0)
    lane = lax.broadcasted_iota(jnp.int32, (size, size), 1)
    return jnp.sum(jnp.where(at == lane, jnp.broadcast_to(row, (size, size)), 0.0), 1, keepdims=True)


def product(a, b, b_axis=0):
    return lax.dot_general(a, b, (((1,), (b_axis,)), ((), ())), preferred_element_type=F32)


def tower_kernel(
    lengths_in, clips_in, assign_in, positives_in, conv_in, proj_in,
    out, proj_w, lengths, clips, assign, positives, conv_w, wide, stacked, sems,
):
    count, frames, channels = clips.shape
    half = frames // 2
    parts = clips.shape[0] // 4
    copies = [pltpu.make_async_copy(lengths_in, lengths, sems.at[0])]
    for n in range(4):
        part = pl.ds(n * parts, parts)
        copies.append(pltpu.make_async_copy(clips_in.at[part], clips.at[part], sems.at[1 + n]))
    copies.append(pltpu.make_async_copy(conv_in, conv_w, sems.at[5]))
    copies.append(pltpu.make_async_copy(assign_in, assign, sems.at[6]))
    copies.append(pltpu.make_async_copy(positives_in, positives, sems.at[7]))
    copies.append(pltpu.make_async_copy(proj_in, proj_w, sems.at[8]))
    for copy in copies[:-1]:
        copy.start()
    wide[:, :, 0:8, :] = jnp.zeros((wide.shape[0], channels // LANES, 8, LANES), F32)
    rows = lax.broadcasted_iota(jnp.int32, (half, 1), 0)
    copies[0].wait()
    for c in range(count):
        if c % parts == 0:
            copies[1 + c // parts].wait()
        inside = 2 * rows + 1 < lengths[c]
        base = c * half
        buffer = wide.at[c % wide.shape[0]]
        for k in range(channels // LANES):
            buffer[k, 8 : 8 + frames, :] = clips[c, :, k * LANES : (k + 1) * LANES].astype(F32)
        for k in range(channels // LANES):
            strip = buffer.at[k]
            taps = (
                strip[pl.ds(7, half, stride=2), :],
                strip[pl.ds(8, half, stride=2), :],
                jnp.where(inside, strip[pl.ds(9, half, stride=2), :], 0.0),
            )
            for tap, values in enumerate(taps):
                first = tap * channels + k * LANES
                stacked[base : base + half, first : first + LANES] = values.astype(BF16)
    copies[-1].start()
    for copy in copies[5:-1]:
        copy.wait()
    pooled = []
    step = parts * half
    for n in range(4):
        hidden = gelu(product(stacked[n * step : (n + 1) * step], conv_w[...]))
        for c in range(parts):
            length = lengths[n * parts + c]
            valid = 2 * rows < length
            total = jnp.sum(
                jnp.where(valid, hidden[c * half : (c + 1) * half], 0.0), axis=0, keepdims=True
            )
            pooled.append(total / ((length + 1) // 2).astype(F32))
    out[:, 0:channels] = jnp.concatenate(pooled, axis=0).astype(BF16)
    slots = as_column(assign[...].astype(F32))
    low = as_column((positives[...] & 255).astype(F32))
    high = as_column((positives[...] >> 8).astype(F32))
    lane = lax.broadcasted_iota(jnp.int32, (count, LANES), 1)
    marks = jnp.where(lane == 0, slots, jnp.where(lane == 1, low, jnp.where(lane == 2, high, 0.0)))
    out[:, channels : channels + LANES] = marks.astype(BF16)
    copies[-1].wait()


def normalized(wide):
    return (wide * lax.rsqrt(jnp.sum(wide * wide, axis=1, keepdims=True) + 1e-06)).astype(BF16)


def weights(logits, hit):
    return jnp.where(hit, -jax.nn.sigmoid(-logits), jax.nn.sigmoid(logits)).astype(BF16)


def embedded(pooled, proj_w):
    return normalized(product(pooled, proj_w[...]))


def pulled_by(scale, bias, texts, audio):
    zt = normalized(texts[texts.shape[0] // 2 :].astype(F32))
    logits = scale[0] * product(zt, audio, 1) + bias[0]
    return scale[0] * product(jax.nn.sigmoid(logits).astype(BF16), audio)


def next_kernel(scale, bias, *refs):
    *blocks, proj_w, texts, audio_out, after_out = refs
    channels = proj_w.shape[0]
    pooled = jnp.concatenate([block[:, 0:channels] for block in blocks], axis=0)
    audio = embedded(pooled, proj_w)
    audio_out[...] = audio
    after_out[...] = pulled_by(scale, bias, texts, audio).astype(BF16)


def own_kernel(scale, bias, *refs):
    *blocks, rows_of, texts, text_out, pair_out = refs
    count, channels = text_out.shape[0], blocks[0].shape[1] - LANES
    blk, sub = lax.axis_index("blk"), lax.axis_index("sub")
    marks = jnp.concatenate([block[:, channels:].astype(F32) for block in blocks], axis=0)
    rows = marks.shape[0]
    column = rows // 2
    audio = rows_of[...]
    slot = marks[:, 0:1].astype(jnp.int32)
    match = marks[:, 1:2] + 256.0 * marks[:, 2:3]
    here = lax.broadcasted_iota(jnp.int32, (rows, 1), 0)
    block = here % column // count
    source = (slot // count ^ sub) * column + block * count + slot % count
    lane = lax.broadcasted_iota(jnp.int32, (rows, rows), 1)
    picked = lane == source
    near = jnp.concatenate([picked[0:count], picked[column : column + count]], axis=0)
    pair_out[...] = product(jnp.where(near, 1.0, 0.0).astype(BF16), audio).astype(BF16)
    wanted_by = jnp.sum(
        jnp.where(picked, jnp.broadcast_to(match, (rows, rows)), 0.0), 0, keepdims=True
    )
    zt = normalized(texts[0:count].astype(F32))
    logits = scale[0] * product(zt, audio, 1) + bias[0]
    at = lax.broadcasted_iota(jnp.int32, (count, 1), 0) + (blk * 2 + sub) * count
    text_out[...] = scale[0] * product(weights(logits, at.astype(F32) == wanted_by), audio)


def pushed_by(bits, start, scale, bias, pair, base, opposite, texts):
    count = pair.shape[0] // 2
    channels = base.shape[1] - LANES
    blk, sub = lax.axis_index("blk"), lax.axis_index("sub")
    marks = jnp.concatenate(
        [base[0:count, channels:], opposite[0:count, channels:]], axis=0
    ).astype(F32)
    match = marks[:, 1:2] + 256.0 * marks[:, 2:3]
    zt = normalized(texts.astype(F32))
    logits = scale[0] * product(pair[...], zt, 1) + bias[0]
    at = lax.broadcasted_iota(jnp.int32, (1, texts.shape[0]), 1) + start
    step = at // count
    away = jnp.zeros_like(at)
    for k, bit in enumerate(bits):
        away = away + ((step >> (k + 1)) & 1) * bit
    wanted = jnp.where((step & 1) == 0, ((blk ^ away) * 2 + sub) * count + at % count, -1)
    return scale[0] * product(weights(logits, wanted.astype(F32) == match), zt)


def audio_kernel(
    bits, scale, bias, pair, everyone, texts, peer_out, audio_out
):
    count = pair.shape[0] // 2
    total = pushed_by(bits, 0, scale, bias, pair, everyone, everyone.at[everyone.shape[0] // 2 :], texts[...])
    peer_out[...] = total[count:].astype(BF16)
    audio_out[...] = total[:count]


def sum_kernel(audio, peer, text, after, audio_grad, text_grad):
    audio_grad[...] = audio[...] + peer[...].astype(F32)
    text_grad[...] = text[...] + after[...].astype(F32)


def in_hbm(array):
    return pltpu.with_memory_space_constraint(array, pltpu.HBM)


def tower(clips, lengths, assign, positives, conv_w, proj_w):
    count, frames, channels = clips.shape
    inputs = (lengths, clips, assign, positives, conv_w, proj_w)
    return pl.pallas_call(
        tower_kernel,
        out_shape=[
            jax.ShapeDtypeStruct((count, channels + LANES), BF16),
            jax.ShapeDtypeStruct(proj_w.shape, BF16),
        ],
        in_specs=[HBM] * 6,
        out_specs=[VMEM] * 2,
        scratch_shapes=[
            pltpu.SMEM(lengths.shape, jnp.int32),
            pltpu.VMEM(clips.shape, BF16),
            pltpu.VMEM(assign.shape, jnp.int32),
            pltpu.VMEM(positives.shape, jnp.int32),
            pltpu.VMEM(conv_w.shape, BF16),
            pltpu.VMEM((2, channels // LANES, 8 + frames, LANES), F32),
            pltpu.VMEM((count * frames // 2, 3 * channels), BF16),
            pltpu.SemaphoreType.DMA((9,)),
        ],
        compiler_params=PARAMS,
        cost_estimate=pl.CostEstimate(
            flops=count * frames * 3 * channels * channels,
            bytes_accessed=clips.size * 4,
            transcendentals=count * frames * channels // 2,
        ),
        name="tower",
    )(*map(in_hbm, inputs))


def on_device(clips, lengths, assign, text, positives, conv_w, proj_w, logit_scale, logit_bias):
    count, frames, channels = clips.shape
    width = text.shape[1]
    assert lax.axis_size("sub") == 2 and count <= 128 and count % 4 == 0
    bits = bits_of(lax.axis_size("blk"))
    before = passed_along(text, "grp", 1)
    own, proj_w = tower(clips, lengths, assign, positives, conv_w, proj_w)
    own, both = lax.optimization_barrier((own, jnp.concatenate([text, before], axis=0)))
    gathered = doubled(own, "blk", bits[:-1])
    gathered, later, logit_scale, logit_bias = lax.optimization_barrier(
        (gathered, both, logit_scale, logit_bias)
    )
    last = bits[-1:]
    corner = swapped_over(gathered, ("blk", "sub"), last + [1])
    beside_it = swapped_over(gathered, ("blk",), last)
    opposite = swapped_over(gathered, ("sub",), [1])
    texts = doubled(both, "blk", bits[:-1])
    farther = texts[2 * count :]
    texts = jnp.concatenate(
        [texts, swapped(later, "blk", bits[-1]), swapped(farther, "blk", bits[-1])], axis=0
    )
    everyone = jnp.concatenate([gathered, beside_it, opposite, corner], axis=0)
    scale, bias = logit_scale.reshape(1), logit_bias.reshape(1)
    block, double = (count, width), (2 * count, width)
    quarter = gathered.shape[0]

    def call(kernel, name, out_shape, *operands):
        return pl.pallas_call(
            kernel,
            out_shape=[jax.ShapeDtypeStruct(shape, kind) for shape, kind in out_shape],
            in_specs=[SMEM, SMEM] + [VMEM] * len(operands),
            out_specs=[VMEM] * len(out_shape),
            compiler_params=PARAMS,
            name=name,
        )(scale, bias, *operands)

    audio, after = call(
        next_kernel, "next_texts",
        [((4 * quarter, width), BF16), (block, BF16)],
        everyone, proj_w, both,
    )
    after = passed_along(after, "grp", -1)
    text_part, pair = call(
        own_kernel, "own_texts",
        [(block, F32), (double, BF16)],
        everyone, audio, both,
    )
    peer, audio_part = call(
        functools.partial(audio_kernel, bits), "audio_side",
        [(block, BF16), (block, F32)],
        pair, everyone, texts,
    )
    peer = swapped(peer, "sub", 1)
    return pl.pallas_call(
        sum_kernel,
        out_shape=[jax.ShapeDtypeStruct(block, F32)] * 2,
        in_specs=[VMEM] * 4,
        out_specs=[VMEM] * 2,
        compiler_params=PARAMS,
        name="sums",
    )(audio_part, peer, text_part, after)


def solution(mesh):
    in_specs = (
        P(("grp", "blk", "sub"), None, None),
        P(("grp", "blk", "sub")),
        P(("grp", "blk"), "sub"),
        P(("grp", "blk", "sub"), None),
        P("grp", ("blk", "sub")),
        P(),
        P(),
        P(),
        P(),
    )
    out_specs = (P(("grp", "blk", "sub"), None), P(("grp", "blk", "sub"), None))
    return jax.shard_map(
        on_device, mesh=mesh, in_specs=in_specs, out_specs=out_specs, check_vma=False
    )
```
